512 devices in a mesh: row: 32 (over x, z), col: 16 (over y, core).
Axes of the slice: x: 4, y: 8, z: 8, core: 2. Of those that a mesh axis runs over, the one named last changes fastest.
Arguments:
- qkv_grad: bfloat16 [8192, 18432], P('row', 'col'), may hold values from -2.5 to 2.5
- qkv_moment: bfloat16 [8192, 18432], P('row', 'col'), may hold values from -256 to 256
- qkv_basis: bfloat16 [18432, 256], P('col', 'row'), may hold values from -6 to 6
- out_grad: bfloat16 [8192, 16384], P('row', 'col'), may hold values from -2.5 to 2.5
- out_moment: bfloat16 [8192, 16384], P('row', 'col'), may hold values from -256 to 256
- out_basis: bfloat16 [16384, 256], P('col', 'row'), may hold values from -6 to 6
Outputs:
- qkv_moment_next: bfloat16 [8192, 18432], P('row', 'col')
- qkv_left: bfloat16 [8192, 256], P('row')
- qkv_right: bfloat16 [18432, 256], P('col', 'row')
- out_moment_next: bfloat16 [8192, 16384], P('row', 'col')
- out_left: bfloat16 [8192, 256], P('row')
- out_right: bfloat16 [16384, 256], P('col', 'row')
The draws below stay inside these ranges and needn't reach their ends.
All inputs are finite; a program needn't handle non-finite values.
Results may differ from the reference program's by a relative error of at most 0.012.
Values may be sent and summed in bfloat16 or wider, within the bound.
No kernel may reach another device: no remote copies, remote signals or barrier semaphores. Data moves between devices by JAX's collectives and lax.ppermute only.
A program may use at most 64 MiB of HBM per device.

```python
import math
import jax
import jax.numpy as jnp
from jax import lax

ROWS = 8192
QKV_COLS = 18432
OUT_COLS = 16384
RANK = 256


def scaled_entries(key, entries, row_spread, row_ramp, col_spread, col_ramp):
    row_count, col_count = entries.shape
    row_key, col_key = jax.random.split(key)
    row_unit = jax.random.uniform(row_key, (row_count, 1), jnp.float32)
    col_unit = jax.random.uniform(col_key, (1, col_count), jnp.float32)
    position = jnp.arange(row_count, dtype=jnp.float32)[:, None] / row_count
    tooth = jnp.mod(2.0 * position, 1.0)
    col_position = jnp.arange(col_count, dtype=jnp.float32)[None, :] / col_count
    row_scale = jnp.exp((row_unit - 0.5) * math.log(row_spread) + (tooth - 0.5) * math.log(row_ramp))
    col_scale = jnp.exp((col_unit - 0.5) * math.log(col_spread) + (col_position - 0.5) * math.log(col_ramp))
    return entries * row_scale * col_scale


def grid_values(values):
    return jnp.floor(jnp.clip(values, -2.99, 2.99) * 64.0) / 64.0


def moment_field(key, col_count):
    entry_key, left_key, right_key, scale_key = jax.random.split(key, 4)
    span = RANK // 2
    entries = jax.random.truncated_normal(entry_key, -5.0, 5.0, (ROWS, col_count), jnp.float32)
    left_raw = jax.random.truncated_normal(left_key, -2.99, 2.99, (ROWS, span), jnp.float32)
    right_raw = jax.random.truncated_normal(right_key, -2.99, 2.99, (span, col_count), jnp.float32)
    row_spread = 4.0
    row_ramp = 5.0
    col_spread = 4.0
    col_ramp = 3.0
    low_rank = jnp.dot(grid_values(left_raw), grid_values(right_raw), precision=lax.Precision.HIGHEST, preferred_element_type=jnp.float32)
    low_rank = low_rank / math.sqrt(span)
    mixed = 0.6 * low_rank + 0.8 * entries
    moment = jnp.clip(scaled_entries(scale_key, mixed, row_spread, row_ramp, col_spread, col_ramp), -256.0, 256.0)
    return moment.astype(jnp.bfloat16)


def draw_qkv_moment(key, part):
    key = jax.random.fold_in(key, 11)
    return moment_field(key, QKV_COLS)


def draw_out_moment(key, part):
    key = jax.random.fold_in(key, 23)
    return moment_field(key, OUT_COLS)


def shard_levels(stream_key, dims, shards, low, largest):
    gain = 1.0
    for axis_at, shards_of in shards:
        steps = jax.random.uniform(jax.random.fold_in(jax.random.fold_in(stream_key, 6), axis_at), (shards_of,), jnp.float32, low / len(shards), largest / len(shards))
        gain = gain * jnp.repeat(jnp.exp(steps), dims[axis_at] // shards_of).reshape((-1,) + (1,) * (len(dims) - 1 - axis_at))
    return gain


def scatter_about(rng, extent, width, limit, pieces=(), kind=jnp.bfloat16):
    values = width * jax.random.normal(rng, extent, jnp.float32)
    if pieces:
        values = values * shard_levels(rng, extent, pieces, -0.22, 0.18)
    return jnp.clip(values, -limit, limit).astype(kind)


def setup_inputs(seed: int = 0) -> dict:
    seeds = jax.random.split(jax.random.key(seed), 7)
    return {
        "qkv_grad": scatter_about(seeds[0], (ROWS, QKV_COLS), 0.25, 2.5, ((0, 32), (1, 16))),
        "qkv_moment": draw_qkv_moment(jax.random.fold_in(seeds[6], 71), 0),
        "qkv_basis": scatter_about(seeds[2], (QKV_COLS, RANK), 1.0, 6.0, ((0, 16), (1, 32))),
        "out_grad": scatter_about(seeds[3], (ROWS, OUT_COLS), 0.25, 2.5, ((0, 32), (1, 16))),
        "out_moment": draw_out_moment(jax.random.fold_in(seeds[6], 71), 0),
        "out_basis": scatter_about(seeds[5], (OUT_COLS, RANK), 1.0, 6.0, ((0, 16), (1, 32))),
    }


MOMENTUM_DECAY = 0.95
EPSILON = 1e-06

def dion_matrix(grad_matrix, moment_matrix, basis_matrix):
    combined = (moment_matrix.astype(jnp.float32) + grad_matrix.astype(jnp.float32)).astype(jnp.bfloat16)
    projection = jnp.dot(combined.astype(jnp.float32), basis_matrix.astype(jnp.float32), preferred_element_type=jnp.float32)
    gram_matrix = jnp.dot(projection.T.astype(jnp.float32), projection.astype(jnp.float32), precision=lax.Precision.HIGHEST, preferred_element_type=jnp.float32) / ROWS
    factor = jnp.linalg.cholesky(gram_matrix)
    left_basis = jax.scipy.linalg.solve_triangular(factor, projection.T, lower=True).T.astype(jnp.bfloat16)
    coefficients = lax.dot_general(combined.astype(jnp.float32), left_basis.astype(jnp.float32), (((0,), (0,)), ((), ())), preferred_element_type=jnp.float32)
    coefficients_low = coefficients.astype(jnp.bfloat16)
    feedback = lax.dot_general(left_basis.astype(jnp.float32), coefficients_low.astype(jnp.float32), (((1,), (1,)), ((), ())), preferred_element_type=jnp.float32)
    moment_next = (combined.astype(jnp.float32) - (1.0 - MOMENTUM_DECAY) / ROWS * feedback).astype(jnp.bfloat16)
    column_mean = lax.optimization_barrier(jnp.mean(coefficients * coefficients, axis=0))
    right_basis = (coefficients / jnp.sqrt(column_mean + EPSILON)[None, :]).astype(jnp.bfloat16)
    return (moment_next, left_basis, right_basis)

def reference(qkv_grad, qkv_moment, qkv_basis, out_grad, out_moment, out_basis):
    qkv_next, qkv_left, qkv_right = dion_matrix(qkv_grad, qkv_moment, qkv_basis)
    out_next, out_left, out_right = dion_matrix(out_grad, out_moment, out_basis)
    return (qkv_next, qkv_left, qkv_right, out_next, out_left, out_right)
```

```python
import functools

import jax
import jax.numpy as jnp
from jax import lax
from jax.experimental import pallas as pl
from jax.experimental.pallas import tpu as pltpu
from jax.sharding import PartitionSpec as P

MOMENTUM_DECAY = 0.95
EPSILON = 1e-06
PANEL = 16
LANES = 128
CORES = 2


def combine_terms(moment_matrix, grad_matrix):
    return (moment_matrix.astype(jnp.float32) + grad_matrix.astype(jnp.float32)).astype(
        jnp.bfloat16
    )


def split_terms(value):
    high = value.astype(jnp.bfloat16)
    rest = value - high.astype(jnp.float32)
    middle = rest.astype(jnp.bfloat16)
    low = (rest - middle.astype(jnp.float32)).astype(jnp.bfloat16)
    return high, middle, low


def whiten_kernel(row_total, gram_ref, proj_ref, left_ref, work_ref):
    size = gram_ref.shape[0]
    rows = proj_ref.shape[0]
    width = size + rows
    work_ref[:, :size] = gram_ref[...] * (1.0 / row_total)
    work_ref[:, size:] = proj_ref[...].T
    row = lax.broadcasted_iota(jnp.int32, (PANEL, LANES), 0)
    for start in range(0, size, PANEL):
        stop = start + PANEL
        base = start // LANES * LANES
        panel = [work_ref[start:stop, at : at + LANES] for at in range(base, width, LANES)]
        columns = [
            jnp.broadcast_to(panel[0][:, at : at + 1], (PANEL, LANES))
            for at in range(start - base, stop - base)
        ]
        pivots = jnp.ones((PANEL, LANES), jnp.float32)
        for step in range(PANEL):
            pivot = jnp.broadcast_to(columns[step][step : step + 1, :], (PANEL, LANES))
            pivots = jnp.where(row == step, pivot, pivots)
            if step == PANEL - 1:
                break
            ratio = jnp.where(row > step, columns[step] * (1.0 / pivot), 0.0)
            for other in range(step + 1, PANEL):
                columns[other] = columns[other] - ratio * columns[other][step : step + 1, :]
            panel = [block - ratio * block[step : step + 1, :] for block in panel]
        scale = lax.rsqrt(pivots)
        scale = scale * (1.5 - 0.5 * pivots * scale * scale)
        panel = [block * scale for block in panel]
        done = (size - base) // LANES
        for at in range(rows // LANES):
            work_ref[start:stop, size + at * LANES : size + (at + 1) * LANES] = panel[done + at]
        if stop < size:
            later = stop // LANES * LANES
            high, middle, low = split_terms(
                jnp.concatenate(panel[(later - base) // LANES :], axis=1)
            )
            keep = size - later
            lhs = jnp.concatenate(
                [part[:, :keep] for part in (high, high, high, middle, middle, low)], axis=0
            )
            rhs = jnp.concatenate([high, middle, low, high, middle, high], axis=0)
            update = lax.dot_general(
                lhs, rhs, (((0,), (0,)), ((), ())), preferred_element_type=jnp.float32
            )
            work_ref[stop:size, later:] = work_ref[stop:size, later:] - update[stop - later :, :]
    left_ref[...] = work_ref[:, size:].T.astype(left_ref.dtype)


def whiten(gram_sum, projection, row_total):
    size = gram_sum.shape[0]
    rows = projection.shape[0]
    return pl.pallas_call(
        functools.partial(whiten_kernel, float(row_total)),
        out_shape=jax.ShapeDtypeStruct((rows, size), jnp.bfloat16),
        in_specs=[pl.BlockSpec(memory_space=pltpu.VMEM)] * 2,
        out_specs=pl.BlockSpec(memory_space=pltpu.VMEM),
        scratch_shapes=[pltpu.VMEM((size, size + rows), jnp.float32)],
        compiler_params=pltpu.CompilerParams(vmem_limit_bytes=32 * 2**20),
    )(gram_sum, projection)


def exchange(blocks, axis, groups=None):
    return lax.all_to_all(blocks, axis, 0, 0, axis_index_groups=groups)


def gather(block, axis, count, groups=None):
    return exchange(jnp.broadcast_to(block[None], (count, *block.shape)), axis, groups)


def scatter_sum(blocks, axis, groups=None):
    return jnp.sum(exchange(blocks, axis, groups).astype(jnp.float32), axis=0)


def per_device(qkv_grad, qkv_moment, qkv_basis, out_grad, out_moment, out_basis):
    row_count = lax.axis_size("row")
    col_count = lax.axis_size("col")
    chips = col_count // CORES
    same_core = [[chip * CORES + core for chip in range(chips)] for core in range(CORES)]
    same_chip = [[chip * CORES + core for core in range(CORES)] for chip in range(chips)]
    local_rows, qkv_width = qkv_grad.shape
    width = qkv_width + out_grad.shape[1]
    row_total = local_rows * row_count
    share = qkv_basis.shape[1]
    rank = share * row_count
    qkv_total = qkv_width * col_count
    out_total = (width - qkv_width) * col_count

    with jax.named_scope("basis_gather"):
        basis = jnp.concatenate([qkv_basis.T, out_basis.T], axis=1)
        basis = gather(basis, "row", row_count).reshape(rank, width)
    with jax.named_scope("projection_partial"):
        qkv_combined = combine_terms(qkv_moment, qkv_grad)
        out_combined = combine_terms(out_moment, out_grad)
        partial = [
            lax.dot_general(
                combined,
                part,
                (((1,), (1,)), ((), ())),
                preferred_element_type=jnp.float32,
            ).reshape(chips, local_rows // chips, rank)
            for combined, part in (
                (qkv_combined, basis[:, :qkv_width]),
                (out_combined, basis[:, qkv_width:]),
            )
        ]
        partial = jnp.stack(partial, axis=1).reshape(col_count, local_rows // chips, rank)
    with jax.named_scope("projection_sum"):
        own = scatter_sum(partial, "col")
        projection = gather(own, "col", chips, same_core).reshape(local_rows, rank)
    with jax.named_scope("gram_sum"):
        gram = jnp.dot(
            projection.T,
            projection,
            precision=lax.Precision.HIGHEST,
            preferred_element_type=jnp.float32,
        )
        gram = scatter_sum(gram.reshape(row_count, share, rank), "row")
        gram = gather(gram, "row", row_count).reshape(rank, rank)
    with jax.named_scope("whiten"):
        left = whiten(gram, projection, row_total)
        left = gather(left, "col", CORES, same_chip)
    qkv_left, out_left = left[0], left[1]
    with jax.named_scope("coefficients"):
        terms = [
            lax.dot_general(
                part, combined, (((0,), (0,)), ((), ())), preferred_element_type=jnp.float32
            ).astype(jnp.bfloat16)
            for part, combined in ((qkv_left, qkv_combined), (out_left, out_combined))
        ]
        terms = jnp.concatenate(terms, axis=1).reshape(row_count, share, width)
        coeff = scatter_sum(terms, "row")
    with jax.named_scope("coefficient_gather"):
        low = gather(coeff.astype(jnp.bfloat16), "row", row_count).reshape(rank, width)
    with jax.named_scope("squares"):
        squared = coeff * coeff
        lane = lax.broadcasted_iota(jnp.int32, (share, LANES), 1)
        squares = jnp.where(
            lane < LANES // 2,
            jnp.sum(squared[:, :qkv_width], axis=1, keepdims=True),
            jnp.sum(squared[:, qkv_width:], axis=1, keepdims=True),
        )
        squares = jnp.sum(gather(squares, "col", col_count), axis=0)
        qkv_scale = jnp.sqrt(squares[:, :1] / qkv_total + EPSILON)
        out_scale = jnp.sqrt(squares[:, LANES // 2 : LANES // 2 + 1] / out_total + EPSILON)
        qkv_right = (coeff[:, :qkv_width] / qkv_scale).astype(jnp.bfloat16).T
        out_right = (coeff[:, qkv_width:] / out_scale).astype(jnp.bfloat16).T
    with jax.named_scope("moment_next"):
        nexts = [
            (
                combined.astype(jnp.float32)
                - (1.0 - MOMENTUM_DECAY)
                / row_total
                * jnp.dot(part, part_low, preferred_element_type=jnp.float32)
            ).astype(jnp.bfloat16)
            for combined, part, part_low in (
                (qkv_combined, qkv_left, low[:, :qkv_width]),
                (out_combined, out_left, low[:, qkv_width:]),
            )
        ]
    return (nexts[0], qkv_left, qkv_right, nexts[1], out_left, out_right)


def solution(mesh):
    placed = (
        P("row", "col"),
        P("row", "col"),
        P("col", "row"),
        P("row", "col"),
        P("row", "col"),
        P("col", "row"),
    )
    return jax.shard_map(
        per_device,
        mesh=mesh,
        in_specs=placed,
        out_specs=(
            P("row", "col"),
            P("row", None),
            P("col", "row"),
            P("row", "col"),
            P("row", None),
            P("col", "row"),
        ),
        check_vma=False,
    )
```

```python
import functools

import jax
import jax.numpy as jnp
from jax import lax
from jax.experimental import pallas as pl
from jax.experimental.pallas import tpu as pltpu
from jax.sharding import PartitionSpec as P

MOMENTUM_DECAY = 0.95
EPSILON = 1e-06
PANEL = 16
LANES = 128
CORES = 2
DEPTH = 8


def combine_terms(moment_matrix, grad_matrix):
    return (moment_matrix.astype(jnp.float32) + grad_matrix.astype(jnp.float32)).astype(
        jnp.bfloat16
    )


def split_terms(value):
    high = value.astype(jnp.bfloat16)
    rest = value - high.astype(jnp.float32)
    middle = rest.astype(jnp.bfloat16)
    low = (rest - middle.astype(jnp.float32)).astype(jnp.bfloat16)
    return high, middle, low


def whiten_kernel(row_total, gram_ref, proj_ref, left_ref, work_ref):
    size = gram_ref.shape[0]
    rows = proj_ref.shape[0]
    width = size + rows
    work_ref[:, :size] = gram_ref[...] * (1.0 / row_total)
    work_ref[:, size:] = proj_ref[...].T
    row = lax.broadcasted_iota(jnp.int32, (PANEL, LANES), 0)
    for start in range(0, size, PANEL):
        stop = start + PANEL
        base = start // LANES * LANES
        panel = [work_ref[start:stop, at : at + LANES] for at in range(base, width, LANES)]
        columns = [
            jnp.broadcast_to(panel[0][:, at : at + 1], (PANEL, LANES))
            for at in range(start - base, stop - base)
        ]
        pivots = jnp.ones((PANEL, LANES), jnp.float32)
        for step in range(PANEL):
            pivot = jnp.broadcast_to(columns[step][step : step + 1, :], (PANEL, LANES))
            pivots = jnp.where(row == step, pivot, pivots)
            if step == PANEL - 1:
                break
            ratio = jnp.where(row > step, columns[step] * (1.0 / pivot), 0.0)
            for other in range(step + 1, PANEL):
                columns[other] = columns[other] - ratio * columns[other][step : step + 1, :]
            panel = [block - ratio * block[step : step + 1, :] for block in panel]
        scale = lax.rsqrt(pivots)
        scale = scale * (1.5 - 0.5 * pivots * scale * scale)
        panel = [block * scale for block in panel]
        done = (size - base) // LANES
        for at in range(rows // LANES):
            work_ref[start:stop, size + at * LANES : size + (at + 1) * LANES] = panel[done + at]
        if stop < size:
            later = stop // LANES * LANES
            high, middle, low = split_terms(
                jnp.concatenate(panel[(later - base) // LANES :], axis=1)
            )
            keep = size - later
            lhs = jnp.concatenate(
                [part[:, :keep] for part in (high, high, high, middle, middle, low)], axis=0
            )
            rhs = jnp.concatenate([high, middle, low, high, middle, high], axis=0)
            update = lax.dot_general(
                lhs, rhs, (((0,), (0,)), ((), ())), preferred_element_type=jnp.float32
            )
            work_ref[stop:size, later:] = work_ref[stop:size, later:] - update[stop - later :, :]
    left_ref[...] = work_ref[:, size:].T.astype(left_ref.dtype)


def whiten(gram_sum, projection, row_total):
    size = gram_sum.shape[0]
    rows = projection.shape[0]
    return pl.pallas_call(
        functools.partial(whiten_kernel, float(row_total)),
        out_shape=jax.ShapeDtypeStruct((rows, size), jnp.bfloat16),
        in_specs=[pl.BlockSpec(memory_space=pltpu.VMEM)] * 2,
        out_specs=pl.BlockSpec(memory_space=pltpu.VMEM),
        scratch_shapes=[pltpu.VMEM((size, size + rows), jnp.float32)],
        compiler_params=pltpu.CompilerParams(vmem_limit_bytes=32 * 2**20),
    )(gram_sum, projection)


def exchange(blocks, axis, groups=None):
    return lax.all_to_all(blocks, axis, 0, 0, axis_index_groups=groups)


def gather(block, axis, count, groups=None):
    return exchange(jnp.broadcast_to(block[None], (count, *block.shape)), axis, groups)


def scatter_sum(blocks, axis, groups=None):
    return jnp.sum(exchange(blocks, axis, groups).astype(jnp.float32), axis=0)


def per_device(qkv_grad, qkv_moment, qkv_basis, out_grad, out_moment, out_basis):
    row_count = lax.axis_size("row")
    col_count = lax.axis_size("col")
    chips = col_count // CORES
    same_core = [[chip * CORES + core for chip in range(chips)] for core in range(CORES)]
    same_chip = [[chip * CORES + core for core in range(CORES)] for chip in range(chips)]
    outer = row_count // DEPTH
    along_z = [[x * DEPTH + z for z in range(DEPTH)] for x in range(outer)]
    along_x = [[x * DEPTH + z for x in range(outer)] for z in range(DEPTH)]
    local_rows, qkv_width = qkv_grad.shape
    width = qkv_width + out_grad.shape[1]
    row_total = local_rows * row_count
    share = qkv_basis.shape[1]
    rank = share * row_count
    qkv_total = qkv_width * col_count
    out_total = (width - qkv_width) * col_count

    with jax.named_scope("basis_gather"):
        basis = jnp.concatenate([qkv_basis.T, out_basis.T], axis=1)
        basis = gather(basis, "row", DEPTH, along_z).reshape(DEPTH * share, width)
        basis = gather(basis, "row", outer, along_x).reshape(rank, width)
    with jax.named_scope("projection_partial"):
        qkv_combined = combine_terms(qkv_moment, qkv_grad)
        out_combined = combine_terms(out_moment, out_grad)
        partial = [
            lax.dot_general(
                combined,
                part,
                (((1,), (1,)), ((), ())),
                preferred_element_type=jnp.float32,
            )
            for combined, part in (
                (qkv_combined, basis[:, :qkv_width]),
                (out_combined, basis[:, qkv_width:]),
            )
        ]
        partial = jnp.stack(partial)
    with jax.named_scope("projection_sum"):
        own = scatter_sum(partial, "col", same_chip)
        own = own.reshape(chips, local_rows // chips, rank)
        own = scatter_sum(own, "col", same_core)
        projection = gather(own, "col", chips, same_core).reshape(local_rows, rank)
    with jax.named_scope("gram_sum"):
        gram = jnp.dot(
            projection.T,
            projection,
            precision=lax.Precision.HIGHEST,
            preferred_element_type=jnp.float32,
        )
        gram = scatter_sum(gram.reshape(row_count, share, rank), "row")
        gram = gather(gram, "row", row_count).reshape(rank, rank)
    with jax.named_scope("whiten"):
        left = whiten(gram, projection, row_total)
        left = gather(left, "col", CORES, same_chip)
    qkv_left, out_left = left[0], left[1]
    with jax.named_scope("coefficients"):
        terms = [
            lax.dot_general(
                part, combined, (((0,), (0,)), ((), ())), preferred_element_type=jnp.float32
            ).astype(jnp.bfloat16)
            for part, combined in ((qkv_left, qkv_combined), (out_left, out_combined))
        ]
        terms = jnp.concatenate(terms, axis=1).reshape(outer, DEPTH * share, width)
        terms = scatter_sum(terms, "row", along_x).astype(jnp.bfloat16)
        coeff = scatter_sum(terms.reshape(DEPTH, share, width), "row", along_z)
    with jax.named_scope("squares"):
        squared = coeff * coeff
        squares = jnp.concatenate(
            [
                jnp.broadcast_to(jnp.sum(part, axis=1, keepdims=True), (share, LANES // 2))
                for part in (squared[:, :qkv_width], squared[:, qkv_width:])
            ],
            axis=1,
        )
        squares = jnp.sum(gather(squares, "col", col_count), axis=0)
        qkv_scale = jnp.sqrt(squares[:, :1] / qkv_total + EPSILON)
        out_scale = jnp.sqrt(squares[:, LANES // 2 : LANES // 2 + 1] / out_total + EPSILON)
        qkv_right = (coeff[:, :qkv_width] / qkv_scale).astype(jnp.bfloat16).T
        out_right = (coeff[:, qkv_width:] / out_scale).astype(jnp.bfloat16).T
    with jax.named_scope("coefficient_gather"):
        low, qkv_right, out_right = lax.optimization_barrier(
            (coeff.astype(jnp.bfloat16), qkv_right, out_right)
        )
        low = gather(low, "row", DEPTH, along_z).reshape(DEPTH * share, width)
        low = gather(low, "row", outer, along_x).reshape(rank, width)
    with jax.named_scope("moment_next"):
        nexts = [
            (
                combined.astype(jnp.float32)
                - (1.0 - MOMENTUM_DECAY)
                / row_total
                * jnp.dot(part, part_low, preferred_element_type=jnp.float32)
            ).astype(jnp.bfloat16)
            for combined, part, part_low in (
                (qkv_combined, qkv_left, low[:, :qkv_width]),
                (out_combined, out_left, low[:, qkv_width:]),
            )
        ]
    return (nexts[0], qkv_left, qkv_right, nexts[1], out_left, out_right)


def solution(mesh):
    placed = (
        P("row", "col"),
        P("row", "col"),
        P("col", "row"),
        P("row", "col"),
        P("row", "col"),
        P("col", "row"),
    )
    return jax.shard_map(
        per_device,
        mesh=mesh,
        in_specs=placed,
        out_specs=(
            P("row", "col"),
            P("row", None),
            P("col", "row"),
            P("row", "col"),
            P("row", None),
            P("col", "row"),
        ),
        check_vma=False,
    )
```

```python
import functools

import jax
import jax.numpy as jnp
from jax import lax
from jax.experimental import pallas as pl
from jax.experimental.pallas import tpu as pltpu
from jax.sharding import PartitionSpec as P

MOMENTUM_DECAY = 0.95
EPSILON = 1e-06
PANEL = 16
LANES = 128
CORES = 2
DEPTH = 8


def combine_terms(moment_matrix, grad_matrix):
    return (moment_matrix.astype(jnp.float32) + grad_matrix.astype(jnp.float32)).astype(
        jnp.bfloat16
    )


def split_terms(value):
    high = value.astype(jnp.bfloat16)
    rest = value - high.astype(jnp.float32)
    middle = rest.astype(jnp.bfloat16)
    low = (rest - middle.astype(jnp.float32)).astype(jnp.bfloat16)
    return high, middle, low


def whiten_kernel(row_total, gram_ref, proj_ref, left_ref, work_ref):
    size = gram_ref.shape[0]
    rows = proj_ref.shape[0]
    width = size + rows
    work_ref[:, :size] = gram_ref[...] * (1.0 / row_total)
    work_ref[:, size:] = proj_ref[...].T
    row = lax.broadcasted_iota(jnp.int32, (PANEL, LANES), 0)
    for start in range(0, size, PANEL):
        stop = start + PANEL
        base = start // LANES * LANES
        panel = [work_ref[start:stop, at : at + LANES] for at in range(base, width, LANES)]
        columns = [
            jnp.broadcast_to(panel[0][:, at : at + 1], (PANEL, LANES))
            for at in range(start - base, stop - base)
        ]
        pivots = jnp.ones((PANEL, LANES), jnp.float32)
        for step in range(PANEL):
            pivot = jnp.broadcast_to(columns[step][step : step + 1, :], (PANEL, LANES))
            pivots = jnp.where(row == step, pivot, pivots)
            if step == PANEL - 1:
                break
            ratio = jnp.where(row > step, columns[step] * (1.0 / pivot), 0.0)
            for other in range(step + 1, PANEL):
                columns[other] = columns[other] - ratio * columns[other][step : step + 1, :]
            panel = [block - ratio * block[step : step + 1, :] for block in panel]
        scale = lax.rsqrt(pivots)
        scale = scale * (1.5 - 0.5 * pivots * scale * scale)
        panel = [block * scale for block in panel]
        done = (size - base) // LANES
        for at in range(rows // LANES):
            work_ref[start:stop, size + at * LANES : size + (at + 1) * LANES] = panel[done + at]
        if stop < size:
            later = stop // LANES * LANES
            high, middle, low = split_terms(
                jnp.concatenate(panel[(later - base) // LANES :], axis=1)
            )
            keep = size - later
            lhs = jnp.concatenate(
                [part[:, :keep] for part in (high, high, high, middle, middle, low)], axis=0
            )
            rhs = jnp.concatenate([high, middle, low, high, middle, high], axis=0)
            update = lax.dot_general(
                lhs, rhs, (((0,), (0,)), ((), ())), preferred_element_type=jnp.float32
            )
            work_ref[stop:size, later:] = work_ref[stop:size, later:] - update[stop - later :, :]
    left_ref[...] = work_ref[:, size:].T.astype(left_ref.dtype)


def whiten(gram_sum, projection, row_total):
    size = gram_sum.shape[0]
    rows = projection.shape[0]
    return pl.pallas_call(
        functools.partial(whiten_kernel, float(row_total)),
        out_shape=jax.ShapeDtypeStruct((rows, size), jnp.bfloat16),
        in_specs=[pl.BlockSpec(memory_space=pltpu.VMEM)] * 2,
        out_specs=pl.BlockSpec(memory_space=pltpu.VMEM),
        scratch_shapes=[pltpu.VMEM((size, size + rows), jnp.float32)],
        compiler_params=pltpu.CompilerParams(vmem_limit_bytes=32 * 2**20),
    )(gram_sum, projection)


def exchange(blocks, axis, groups=None):
    return lax.all_to_all(blocks, axis, 0, 0, axis_index_groups=groups)


def gather(block, axis, count, groups=None):
    return exchange(jnp.broadcast_to(block[None], (count, *block.shape)), axis, groups)


def scatter_sum(blocks, axis, groups=None):
    return jnp.sum(exchange(blocks, axis, groups).astype(jnp.float32), axis=0)


def finish_kernel(scale, count, *refs):
    moments, grads, lefts, blocks = refs[0:2], refs[2:4], refs[4:6], refs[6 : 6 + count]
    nexts, low_ref = refs[6 + count : 8 + count], refs[8 + count]
    depth = blocks[0].shape[0]
    for at, block in enumerate(blocks):
        low_ref[at * depth : (at + 1) * depth, :] = block[...]
    base = 0
    for moment, grad, left, result in zip(moments, grads, lefts, nexts):
        wide = moment.shape[1]
        tile = next(size for size in (512, 384, 256, 128, wide) if wide % size == 0)
        for at in range(0, wide, tile):
            feedback = jnp.dot(
                left[...],
                low_ref[:, base + at : base + at + tile],
                preferred_element_type=jnp.float32,
            )
            combined = combine_terms(moment[:, at : at + tile], grad[:, at : at + tile])
            result[:, at : at + tile] = (
                combined.astype(jnp.float32) - scale * feedback
            ).astype(jnp.bfloat16)
        base += wide


def finish(moments, grads, lefts, blocks, row_total):
    rank = lefts[0].shape[1]
    width = blocks[0].shape[1]
    rows = moments[0].shape[0]
    return pl.pallas_call(
        functools.partial(
            finish_kernel, (1.0 - MOMENTUM_DECAY) / row_total, len(blocks)
        ),
        out_shape=[jax.ShapeDtypeStruct(moment.shape, jnp.bfloat16) for moment in moments],
        in_specs=[pl.BlockSpec(memory_space=pltpu.VMEM)] * (6 + len(blocks)),
        out_specs=[pl.BlockSpec(memory_space=pltpu.VMEM)] * 2,
        scratch_shapes=[pltpu.VMEM((rank, width), jnp.bfloat16)],
        compiler_params=pltpu.CompilerParams(vmem_limit_bytes=32 * 2**20),
        cost_estimate=pl.CostEstimate(
            flops=2 * rows * rank * width,
            bytes_accessed=8 * rows * width,
            transcendentals=0,
        ),
    )(*moments, *grads, *lefts, *blocks)


def per_device(qkv_grad, qkv_moment, qkv_basis, out_grad, out_moment, out_basis):
    row_count = lax.axis_size("row")
    col_count = lax.axis_size("col")
    chips = col_count // CORES
    same_core = [[chip * CORES + core for chip in range(chips)] for core in range(CORES)]
    same_chip = [[chip * CORES + core for core in range(CORES)] for chip in range(chips)]
    outer = row_count // DEPTH
    along_z = [[x * DEPTH + z for z in range(DEPTH)] for x in range(outer)]
    along_x = [[x * DEPTH + z for x in range(outer)] for z in range(DEPTH)]
    local_rows, qkv_width = qkv_grad.shape
    width = qkv_width + out_grad.shape[1]
    row_total = local_rows * row_count
    share = qkv_basis.shape[1]
    rank = share * row_count
    qkv_total = qkv_width * col_count
    out_total = (width - qkv_width) * col_count

    with jax.named_scope("basis_gather"):
        basis = jnp.concatenate([qkv_basis.T, out_basis.T], axis=1)
        basis = gather(basis, "row", DEPTH, along_z).reshape(DEPTH * share, width)
        basis = gather(basis, "row", outer, along_x).reshape(rank, width)
    with jax.named_scope("projection_partial"):
        qkv_combined = combine_terms(qkv_moment, qkv_grad)
        out_combined = combine_terms(out_moment, out_grad)
        partial = [
            lax.dot_general(
                combined,
                part,
                (((1,), (1,)), ((), ())),
                preferred_element_type=jnp.float32,
            )
            for combined, part in (
                (qkv_combined, basis[:, :qkv_width]),
                (out_combined, basis[:, qkv_width:]),
            )
        ]
        partial = jnp.stack(partial)
    with jax.named_scope("projection_sum"):
        own = scatter_sum(partial, "col", same_chip)
        own = own.reshape(chips, local_rows // chips, rank)
        own = scatter_sum(own, "col", same_core)
        projection = gather(own, "col", chips, same_core).reshape(local_rows, rank)
    with jax.named_scope("gram_sum"):
        gram = jnp.dot(
            projection.T,
            projection,
            precision=lax.Precision.HIGHEST,
            preferred_element_type=jnp.float32,
        )
        gram = scatter_sum(gram.reshape(row_count, share, rank), "row")
        gram = gather(gram, "row", row_count).reshape(rank, rank)
    with jax.named_scope("whiten"):
        left = whiten(gram, projection, row_total)
        left = lax.all_gather(left, "col", axis_index_groups=same_chip)
    qkv_left, out_left = left[0], left[1]
    with jax.named_scope("coefficients"):
        terms = [
            lax.dot_general(
                part, combined, (((0,), (0,)), ((), ())), preferred_element_type=jnp.float32
            ).astype(jnp.bfloat16)
            for part, combined in ((qkv_left, qkv_combined), (out_left, out_combined))
        ]
        terms = jnp.concatenate(terms, axis=1).reshape(outer, DEPTH * share, width)
        terms = scatter_sum(terms, "row", along_x).astype(jnp.bfloat16)
        coeff = scatter_sum(terms.reshape(DEPTH, share, width), "row", along_z)
    with jax.named_scope("coefficient_gather_z"):
        low = gather(coeff.astype(jnp.bfloat16), "row", DEPTH, along_z)
        low = low.reshape(DEPTH * share, width)
    with jax.named_scope("coefficient_gather_x"):
        blocks = [low] + [
            lax.ppermute(
                low,
                "row",
                [
                    (x * DEPTH + z, (x - step) % outer * DEPTH + z)
                    for x in range(outer)
                    for z in range(DEPTH)
                ],
            )
            for step in range(1, outer)
        ]
        turn = lax.axis_index("row") // DEPTH * (DEPTH * share)
        turned = [
            lax.dynamic_slice_in_dim(jnp.concatenate([part, part], axis=1), turn, rank, 1)
            for part in (qkv_left, out_left)
        ]
    with jax.named_scope("squares"):
        blocks[1], coeff = lax.optimization_barrier((blocks[1], coeff))
        squared = coeff * coeff
        squares = jnp.concatenate(
            [
                jnp.broadcast_to(jnp.sum(part, axis=1, keepdims=True), (share, LANES // 2))
                for part in (squared[:, :qkv_width], squared[:, qkv_width:])
            ],
            axis=1,
        )
        squares = jnp.sum(gather(squares, "col", col_count), axis=0)
        qkv_scale = jnp.sqrt(squares[:, :1] / qkv_total + EPSILON)
        out_scale = jnp.sqrt(squares[:, LANES // 2 : LANES // 2 + 1] / out_total + EPSILON)
        qkv_right = (coeff[:, :qkv_width] / qkv_scale).astype(jnp.bfloat16).T
        out_right = (coeff[:, qkv_width:] / out_scale).astype(jnp.bfloat16).T
    with jax.named_scope("moment_next"):
        nexts = finish(
            (qkv_moment, out_moment), (qkv_grad, out_grad), turned, blocks, row_total
        )
    return (nexts[0], qkv_left, qkv_right, nexts[1], out_left, out_right)


def solution(mesh):
    placed = (
        P("row", "col"),
        P("row", "col"),
        P("col", "row"),
        P("row", "col"),
        P("row", "col"),
        P("col", "row"),
    )
    return jax.shard_map(
        per_device,
        mesh=mesh,
        in_specs=placed,
        out_specs=(
            P("row", "col"),
            P("row", None),
            P("col", "row"),
            P("row", "col"),
            P("row", None),
            P("col", "row"),
        ),
        check_vma=False,
    )
```

```python
import functools

import jax
import jax.numpy as jnp
from jax import lax
from jax.experimental import pallas as pl
from jax.experimental.pallas import tpu as pltpu
from jax.sharding import PartitionSpec as P

MOMENTUM_DECAY = 0.95
EPSILON = 1e-06
PANEL = 16
LANES = 128
CORES = 2
DEPTH = 8


def combine_terms(moment_matrix, grad_matrix):
    return (moment_matrix.astype(jnp.float32) + grad_matrix.astype(jnp.float32)).astype(
        jnp.bfloat16
    )


def split_terms(value):
    high = value.astype(jnp.bfloat16)
    rest = value - high.astype(jnp.float32)
    middle = rest.astype(jnp.bfloat16)
    low = (rest - middle.astype(jnp.float32)).astype(jnp.bfloat16)
    return high, middle, low


def whiten_kernel(row_total, top_ref, corner_ref, proj_ref, left_ref, work_ref):
    half, size = top_ref.shape
    rows = proj_ref.shape[0]
    width = size + rows
    work_ref[:half, :size] = top_ref[...] * (1.0 / row_total)
    work_ref[half:size, half:size] = corner_ref[...] * (1.0 / row_total)
    work_ref[half:size, :half] = jnp.zeros((size - half, half), jnp.float32)
    work_ref[:, size:] = proj_ref[...].T
    row = lax.broadcasted_iota(jnp.int32, (PANEL, LANES), 0)
    for start in range(0, size, PANEL):
        stop = start + PANEL
        base = start // LANES * LANES
        panel = [work_ref[start:stop, at : at + LANES] for at in range(base, width, LANES)]
        columns = [
            jnp.broadcast_to(panel[0][:, at : at + 1], (PANEL, LANES))
            for at in range(start - base, stop - base)
        ]
        pivots = jnp.ones((PANEL, LANES), jnp.float32)
        for step in range(PANEL):
            pivot = jnp.broadcast_to(columns[step][step : step + 1, :], (PANEL, LANES))
            pivots = jnp.where(row == step, pivot, pivots)
            if step == PANEL - 1:
                break
            ratio = jnp.where(row > step, columns[step] * (1.0 / pivot), 0.0)
            for other in range(step + 1, PANEL):
                columns[other] = columns[other] - ratio * columns[other][step : step + 1, :]
            panel = [block - ratio * block[step : step + 1, :] for block in panel]
        scale = lax.rsqrt(pivots)
        scale = scale * (1.5 - 0.5 * pivots * scale * scale)
        panel = [block * scale for block in panel]
        done = (size - base) // LANES
        for at in range(rows // LANES):
            work_ref[start:stop, size + at * LANES : size + (at + 1) * LANES] = panel[done + at]
        if stop < size:
            later = stop // LANES * LANES
            high, middle, low = split_terms(
                jnp.concatenate(panel[(later - base) // LANES :], axis=1)
            )
            keep = size - later
            lhs = jnp.concatenate(
                [part[:, :keep] for part in (high, high, high, middle, middle, low)], axis=0
            )
            rhs = jnp.concatenate([high, middle, low, high, middle, high], axis=0)
            update = lax.dot_general(
                lhs, rhs, (((0,), (0,)), ((), ())), preferred_element_type=jnp.float32
            )
            work_ref[stop:size, later:] = work_ref[stop:size, later:] - update[stop - later :, :]
    left_ref[...] = work_ref[:, size:].T.astype(left_ref.dtype)


def whiten(top, corner, projection, row_total):
    size = top.shape[1]
    rows = projection.shape[0]
    return pl.pallas_call(
        functools.partial(whiten_kernel, float(row_total)),
        out_shape=jax.ShapeDtypeStruct((rows, size), jnp.bfloat16),
        in_specs=[pl.BlockSpec(memory_space=pltpu.VMEM)] * 3,
        out_specs=pl.BlockSpec(memory_space=pltpu.VMEM),
        scratch_shapes=[pltpu.VMEM((size, size + rows), jnp.float32)],
        compiler_params=pltpu.CompilerParams(vmem_limit_bytes=32 * 2**20),
    )(top, corner, projection)


def exchange(blocks, axis, groups=None):
    return lax.all_to_all(blocks, axis, 0, 0, axis_index_groups=groups)


def gather(block, axis, count, groups=None):
    return exchange(jnp.broadcast_to(block[None], (count, *block.shape)), axis, groups)


def scatter_sum(blocks, axis, groups=None):
    return jnp.sum(exchange(blocks, axis, groups).astype(jnp.float32), axis=0)


def finish_kernel(scale, count, *refs):
    moments, grads, lefts, blocks = refs[0:2], refs[2:4], refs[4:6], refs[6 : 6 + count]
    nexts, low_ref = refs[6 + count : 8 + count], refs[8 + count]
    depth = blocks[0].shape[0]
    for at, block in enumerate(blocks):
        low_ref[at * depth : (at + 1) * depth, :] = block[...]
    base = 0
    for moment, grad, left, result in zip(moments, grads, lefts, nexts):
        wide = moment.shape[1]
        tile = next(size for size in (512, 384, 256, 128, wide) if wide % size == 0)
        for at in range(0, wide, tile):
            feedback = jnp.dot(
                left[...],
                low_ref[:, base + at : base + at + tile],
                preferred_element_type=jnp.float32,
            )
            combined = combine_terms(moment[:, at : at + tile], grad[:, at : at + tile])
            result[:, at : at + tile] = (
                combined.astype(jnp.float32) - scale * feedback
            ).astype(jnp.bfloat16)
        base += wide


def finish(moments, grads, lefts, blocks, row_total):
    rank = lefts[0].shape[1]
    width = blocks[0].shape[1]
    rows = moments[0].shape[0]
    return pl.pallas_call(
        functools.partial(
            finish_kernel, (1.0 - MOMENTUM_DECAY) / row_total, len(blocks)
        ),
        out_shape=[jax.ShapeDtypeStruct(moment.shape, jnp.bfloat16) for moment in moments],
        in_specs=[pl.BlockSpec(memory_space=pltpu.VMEM)] * (6 + len(blocks)),
        out_specs=[pl.BlockSpec(memory_space=pltpu.VMEM)] * 2,
        scratch_shapes=[pltpu.VMEM((rank, width), jnp.bfloat16)],
        compiler_params=pltpu.CompilerParams(vmem_limit_bytes=32 * 2**20),
        cost_estimate=pl.CostEstimate(
            flops=2 * rows * rank * width,
            bytes_accessed=8 * rows * width,
            transcendentals=0,
        ),
    )(*moments, *grads, *lefts, *blocks)


def per_device(qkv_grad, qkv_moment, qkv_basis, out_grad, out_moment, out_basis):
    row_count = lax.axis_size("row")
    col_count = lax.axis_size("col")
    chips = col_count // CORES
    same_core = [[chip * CORES + core for chip in range(chips)] for core in range(CORES)]
    same_chip = [[chip * CORES + core for core in range(CORES)] for chip in range(chips)]
    outer = row_count // DEPTH
    along_z = [[x * DEPTH + z for z in range(DEPTH)] for x in range(outer)]
    along_x = [[x * DEPTH + z for x in range(outer)] for z in range(DEPTH)]
    local_rows, qkv_width = qkv_grad.shape
    width = qkv_width + out_grad.shape[1]
    row_total = local_rows * row_count
    share = qkv_basis.shape[1]
    rank = share * row_count
    qkv_total = qkv_width * col_count
    out_total = (width - qkv_width) * col_count

    with jax.named_scope("basis_gather"):
        basis = jnp.concatenate([qkv_basis.T, out_basis.T], axis=1)
        basis = gather(basis, "row", DEPTH, along_z).reshape(DEPTH * share, width)
        basis = gather(basis, "row", outer, along_x).reshape(rank, width)
    with jax.named_scope("projection_partial"):
        qkv_combined = combine_terms(qkv_moment, qkv_grad)
        out_combined = combine_terms(out_moment, out_grad)
        partial = [
            lax.dot_general(
                combined,
                part,
                (((1,), (1,)), ((), ())),
                preferred_element_type=jnp.float32,
            )
            for combined, part in (
                (qkv_combined, basis[:, :qkv_width]),
                (out_combined, basis[:, qkv_width:]),
            )
        ]
    with jax.named_scope("projection_sum"):
        first = lax.axis_index("col") % CORES == 0
        other = lax.ppermute(
            jnp.where(first, partial[1], partial[0]),
            "col",
            [(source, source ^ 1) for source in range(col_count)],
        )
        own = jnp.where(first, partial[0], partial[1]) + other
        own = own.reshape(chips, local_rows // chips, rank)
        own = scatter_sum(own, "col", same_core)
        projection = gather(own, "col", chips, same_core).reshape(local_rows, rank)
    with jax.named_scope("gram_sum"):
        gram = jnp.dot(
            projection.T,
            projection,
            precision=lax.Precision.HIGHEST,
            preferred_element_type=jnp.float32,
        )
        half = rank // 2
        packed = jnp.concatenate(
            [
                gram[:half].reshape(row_count, half // row_count, rank),
                gram[half:, half:].reshape(row_count, half // row_count, half),
            ],
            axis=2,
        )
        packed = gather(scatter_sum(packed, "row"), "row", row_count)
        top = packed[:, :, :rank].reshape(half, rank)
        corner = packed[:, :, rank:].reshape(half, half)
    with jax.named_scope("whiten"):
        left = whiten(top, corner, projection, row_total)
        left = lax.all_gather(left, "col", axis_index_groups=same_chip)
    qkv_left, out_left = left[0], left[1]
    with jax.named_scope("coefficients"):
        terms = [
            lax.dot_general(
                part, combined, (((0,), (0,)), ((), ())), preferred_element_type=jnp.float32
            ).astype(jnp.bfloat16)
            for part, combined in ((qkv_left, qkv_combined), (out_left, out_combined))
        ]
        terms = jnp.concatenate(terms, axis=1).reshape(outer, DEPTH * share, width)
        terms = scatter_sum(terms, "row", along_x).astype(jnp.bfloat16)
        coeff = scatter_sum(terms.reshape(DEPTH, share, width), "row", along_z)
    with jax.named_scope("coefficient_gather_z"):
        low = gather(coeff.astype(jnp.bfloat16), "row", DEPTH, along_z)
        low = low.reshape(DEPTH * share, width)
    with jax.named_scope("coefficient_gather_x"):
        blocks = [low] + [
            lax.ppermute(
                low,
                "row",
                [
                    (x * DEPTH + z, (x - step) % outer * DEPTH + z)
                    for x in range(outer)
                    for z in range(DEPTH)
                ],
            )
            for step in range(1, outer)
        ]
        turn = lax.axis_index("row") // DEPTH * (DEPTH * share)
        turned = [
            lax.dynamic_slice_in_dim(jnp.concatenate([part, part], axis=1), turn, rank, 1)
            for part in (qkv_left, out_left)
        ]
    with jax.named_scope("squares"):
        blocks[1], coeff = lax.optimization_barrier((blocks[1], coeff))
        squared = coeff * coeff
        squares = jnp.concatenate(
            [
                jnp.broadcast_to(jnp.sum(part, axis=1, keepdims=True), (share, LANES // 2))
                for part in (squared[:, :qkv_width], squared[:, qkv_width:])
            ],
            axis=1,
        )
        squares = jnp.sum(gather(squares, "col", col_count), axis=0)
        qkv_scale = jnp.sqrt(squares[:, :1] / qkv_total + EPSILON)
        out_scale = jnp.sqrt(squares[:, LANES // 2 : LANES // 2 + 1] / out_total + EPSILON)
        qkv_right = (coeff[:, :qkv_width] / qkv_scale).astype(jnp.bfloat16).T
        out_right = (coeff[:, qkv_width:] / out_scale).astype(jnp.bfloat16).T
    with jax.named_scope("moment_next"):
        nexts = finish(
            (qkv_moment, out_moment), (qkv_grad, out_grad), turned, blocks, row_total
        )
    return (nexts[0], qkv_left, qkv_right, nexts[1], out_left, out_right)


def solution(mesh):
    placed = (
        P("row", "col"),
        P("row", "col"),
        P("col", "row"),
        P("row", "col"),
        P("row", "col"),
        P("col", "row"),
    )
    return jax.shard_map(
        per_device,
        mesh=mesh,
        in_specs=placed,
        out_specs=(
            P("row", "col"),
            P("row", None),
            P("col", "row"),
            P("row", "col"),
            P("row", None),
            P("col", "row"),
        ),
        check_vma=False,
    )
```
